32 devices in a mesh: groups: 2 (over y), seq: 4 (over z), tensor: 2 (over x), sub: 2 (over core).
Axes of the slice: x: 2, y: 2, z: 4, core: 2. Of those that a mesh axis runs over, the one named last changes fastest.
Arguments:
- layer_input: bfloat16 [3072, 8192], P(('groups', 'seq'), ('tensor', 'sub')), parts along dimension 0, may hold values from -6 to 6
- out_grad: bfloat16 [3072, 2, 1024], P(('groups', 'seq')), parts along dimension 0, may hold values from -6 to 6
- base_weight: bfloat16 [2048, 8192], P('seq', ('tensor', 'sub')), may hold values from -0.125 to 0.125
- adapter_mid: bfloat16 [3072, 128], P(('groups', 'seq')), parts along dimension 0, may hold values from -0.29882812 to 0.29882812
- adapter_down: bfloat16 [16, 8192, 128], P(('groups', 'seq'), ('tensor', 'sub')), parts along dimension 0, may hold values from -0.75 to 0.75
- adapter_up: bfloat16 [16, 2, 64, 1024], P(('groups', 'seq'), None, None, ('tensor', 'sub')), parts along dimension 0, may hold values from -0.005859375 to 0.005859375
- tenant_counts: int32 [16], P('groups'), parts along dimension 0, may hold values from 1 to 384, as said below
- seg_starts: int32 [16], P('groups'), parts along dimension 0, may hold values from 0 to 1408, as said below
- owner_slot: int32 [16], P('groups'), parts along dimension 0, may hold values from 0 to 7, as said below
Outputs:
- grad_input: bfloat16 [3072, 8192], P(('groups', 'seq'), ('tensor', 'sub')), parts along dimension 0
- grad_down: bfloat16 [16, 8192, 128], P(('groups', 'seq'), ('tensor', 'sub')), parts along dimension 0
- up_adapter_gradient: bfloat16 [16, 2, 64, 1024], P(('groups', 'seq'), None, None, ('tensor', 'sub')), parts along dimension 0
The draws below stay inside these ranges and needn't reach their ends.
There are 2 independent parts, one for each index of `groups`. The reference program is written for one: setup_inputs(seed, part) draws one part's arguments, and reference() takes and returns one part's arrays. A program takes and returns all parts, laid end to end along the dimension named above; an argument that names none is the same for every part. Nothing has to cross between parts.
Inputs may be any that keep to these rules, and one draw needn't show every extreme that they name: Tenants lie in the batch in the order 0 to 7; each segment is a whole number of blocks of 128 rows, ceil(tenant_counts[t] / 128) of them, and only its first tenant_counts[t] rows are live; the busiest tenant has 384 live rows (3 full blocks), and no tenant has more. seg_starts[0] = 0; seg_starts rises by the segments' padded lengths, and the last segment ends at row 1536. owner_slot is owner_slot is a permutation; tenant t's rows of the adapter arrays and gradients are row owner_slot[t], held by seq index owner_slot[t] // 2; that index depends only on t mod (4) and differs between different values of it, and owner_slot[t] mod 2 = t // 4.
All inputs are finite; a program needn't handle non-finite values.
Results may differ from the reference program's by a relative error of at most 0.0049.
Values may be sent and summed in bfloat16 or wider, within the bound.
A program may use at most 128 MiB of HBM per device.

```python
import jax
import jax.numpy as jnp
from jax import lax

D = 8192
KV = 1024
R = 64
BLK = 128
TOK_DEV = 384
TEN_DEV = 2
TOKENS = 1536
TENANTS = 8


def tenant_layout(key):
    seq_count = TENANTS // TEN_DEV
    blk_dev = TOK_DEV // BLK
    blocks = blk_dev * seq_count
    spare_blocks = blocks - TENANTS
    most_blocks = min(blk_dev, 1 + spare_blocks)
    rest_blocks = spare_blocks - (most_blocks - 1)
    subkeys = jax.random.split(jax.random.fold_in(key, 11), 3)
    shuffle = jax.random.permutation(subkeys[0], TENANTS)
    others = shuffle[1:]
    offset = jax.random.randint(subkeys[1], (), 0, TENANTS - 1)
    spread = (jnp.arange(rest_blocks, dtype=jnp.int32) + offset) % (TENANTS - 1)
    extra = jnp.zeros((TENANTS,), jnp.int32).at[shuffle[0]].add(most_blocks - 1)
    extra = extra.at[others[spread]].add(1)
    per_tenant = 1 + extra
    starts = BLK * (jnp.cumsum(per_tenant) - per_tenant)
    last_fill = jax.random.randint(subkeys[2], (TENANTS,), 1, BLK + 1)
    is_busiest = jnp.arange(TENANTS, dtype=jnp.int32) == shuffle[0]
    last_fill = jnp.where(is_busiest, BLK, last_fill)
    counts = (per_tenant - 1) * BLK + last_fill
    return (counts.astype(jnp.int32), starts.astype(jnp.int32))


def draw_tenant_counts(key, part):
    counts, starts = tenant_layout(key)
    return counts


def draw_seg_starts(key, part):
    counts, starts = tenant_layout(key)
    return starts


def draw_owner_slot(key, part):
    key = jax.random.fold_in(key, 3)
    seq_count = TENANTS // TEN_DEV
    owners = jax.random.permutation(key, seq_count)
    tenant_ids = jnp.arange(TENANTS, dtype=jnp.int32)
    return (owners[tenant_ids % seq_count] * TEN_DEV + tenant_ids // seq_count).astype(jnp.int32)


def levels(rng, extent, shards, smallest, largest):
    def one(dim, blocks):
        steps = jax.random.uniform(jax.random.fold_in(jax.random.fold_in(rng, 6), dim), (blocks,), jnp.float32, smallest / len(shards), largest / len(shards))
        return jnp.repeat(jnp.exp(steps), extent[dim] // blocks).reshape((-1,) + (1,) * (len(extent) - dim - 1))

    factor_of = one(*shards[0])
    for cut in shards[1:]:
        factor_of = factor_of * one(*cut)
    return factor_of


def normal_values(key, extent, scale, most, cuts=(), held_as=jnp.bfloat16):
    gain = levels(key, extent, cuts, -0.22, 0.18) if cuts else 1.0
    values = jax.random.normal(key, extent, jnp.float32) * scale * gain
    return jnp.minimum(jnp.maximum(values, -most), most).astype(held_as)


def setup_inputs(seed: int = 0, part: int = 0) -> dict:
    seeds = jax.random.split(jax.random.key(seed), 10)
    own_keys = jax.random.split(jax.random.fold_in(seeds[9], part), 10)
    return {
        "layer_input": normal_values(own_keys[0], (TOKENS, D), 1.0, 6.0, ((0, 4), (1, 4))),
        "out_grad": normal_values(own_keys[1], (TOKENS, 2, KV), 1.0, 6.0, ((0, 4),)),
        "base_weight": normal_values(seeds[2], (2 * KV, D), (2 * KV) ** -0.5, 0.125, ((0, 4), (1, 4))),
        "adapter_mid": normal_values(own_keys[3], (TOKENS, 2 * R), 0.05, 0.29882812, ((0, 4),)),
        "adapter_down": normal_values(own_keys[4], (TENANTS, D, 2 * R), R ** -0.5, 0.75, ((0, 4), (1, 4))),
        "adapter_up": normal_values(own_keys[5], (TENANTS, 2, R, KV), (KV * 1024) ** -0.5, 0.005859375, ((0, 4), (3, 4))),
        "tenant_counts": draw_tenant_counts(jax.random.fold_in(jax.random.fold_in(seeds[9], part), 71), part),
        "seg_starts": draw_seg_starts(jax.random.fold_in(jax.random.fold_in(seeds[9], part), 71), part),
        "owner_slot": draw_owner_slot(jax.random.fold_in(jax.random.fold_in(seeds[9], part), 71), part),
    }


adapter_scale_factor = 2.0


def tenant_tables(tenant_counts, seg_starts, owner_slot, blocks):
    tenant_ids = jnp.arange(owner_slot.shape[0], dtype=jnp.int32)
    block_first = jnp.arange(blocks, dtype=jnp.int32) * BLK
    block_tenant = jnp.sum((seg_starts[None, :] <= block_first[:, None]).astype(jnp.int32), axis=1) - 1
    tenant_hit = block_tenant[:, None] == tenant_ids[None, :]

    def per_block(values):
        return jnp.sum(jnp.where(tenant_hit, values[None, :], 0), axis=1).astype(jnp.int32)

    return block_first, block_tenant, per_block(seg_starts), per_block(tenant_counts), per_block(owner_slot)


def reference(layer_input, out_grad, base_weight, adapter_mid, adapter_down, adapter_up, tenant_counts, seg_starts, owner_slot):
    highest_precision_mode = lax.Precision.HIGHEST
    blocks = TOKENS // BLK
    block_first, block_tenant, start_all, count_all, slot_all = tenant_tables(tenant_counts, seg_starts, owner_slot, blocks)
    offsets = block_first[:, None] + jnp.arange(BLK, dtype=jnp.int32)[None, :] - start_all[:, None]
    live_rows = offsets < count_all[:, None]
    masked = jnp.where(live_rows.reshape(TOKENS, 1, 1), out_grad, jnp.zeros_like(out_grad))
    base_term = jnp.dot(masked.reshape(TOKENS, 2 * KV), base_weight, preferred_element_type=jnp.float32)
    adapter_slot_choice = (slot_all[:, None] == jnp.arange(TENANTS, dtype=jnp.int32)[None, :]).astype(jnp.float32)
    up_projection_blocks = jnp.einsum("bt,tjrk->bjrk", adapter_slot_choice, adapter_up.astype(jnp.float32), precision=highest_precision_mode)
    gradient_block_list = masked.reshape(blocks, BLK, 2, KV).astype(jnp.float32)
    reduced_rank_values = (adapter_scale_factor * jnp.einsum("zpex,zehx->zpeh", gradient_block_list, up_projection_blocks, precision=highest_precision_mode)).astype(jnp.bfloat16)
    reduced_float_type = reduced_rank_values.reshape(blocks, BLK, 2 * R).astype(jnp.float32)
    mid_blocks = adapter_mid.reshape(blocks, BLK, 2, R).astype(jnp.float32)
    up_projection_share = jnp.einsum("bqjr,bqjk->bjrk", mid_blocks, gradient_block_list, precision=highest_precision_mode)
    up_adapter_gradient = (adapter_scale_factor * jnp.einsum("on,olqp->nlqp", adapter_slot_choice, up_projection_share, precision=highest_precision_mode)).astype(jnp.bfloat16)
    input_block_list = layer_input.reshape(blocks, BLK, D).astype(jnp.float32)
    down_projection_share = jnp.einsum("msj,msw->mjw", input_block_list, reduced_float_type, precision=highest_precision_mode)
    grad_down = jnp.einsum("bt,bdr->tdr", adapter_slot_choice, down_projection_share, precision=highest_precision_mode).astype(jnp.bfloat16)
    down_projection_blocks = jnp.einsum("bt,tdr->bdr", adapter_slot_choice, adapter_down.astype(jnp.float32), precision=highest_precision_mode)
    adapter_side_term = jnp.einsum("mjw,mow->mjo", reduced_float_type, down_projection_blocks, precision=highest_precision_mode).astype(jnp.bfloat16)
    grad_input = (base_term + adapter_side_term.reshape(TOKENS, D).astype(jnp.float32)).astype(jnp.bfloat16)
    return (grad_input, grad_down, up_adapter_gradient)
```

```python
import functools

import jax
import jax.numpy as jnp
from jax import lax
from jax.experimental import pallas as pl
from jax.experimental.pallas import tpu as pltpu
from jax.sharding import PartitionSpec as P

BLK = 128


adapter_scale_factor = 2.0


def tenant_tables(tenant_counts, seg_starts, owner_slot, blocks):
    tenant_ids = jnp.arange(owner_slot.shape[0], dtype=jnp.int32)
    block_first = jnp.arange(blocks, dtype=jnp.int32) * BLK
    block_tenant = (
        jnp.sum((seg_starts[None, :] <= block_first[:, None]).astype(jnp.int32), axis=1) - 1
    )
    tenant_hit = block_tenant[:, None] == tenant_ids[None, :]

    def per_block(values):
        return jnp.sum(jnp.where(tenant_hit, values[None, :], 0), axis=1)

    return (
        block_first,
        block_tenant,
        per_block(seg_starts),
        per_block(tenant_counts),
        per_block(owner_slot),
    )


def local(
    layer_input,
    out_grad,
    base_weight,
    adapter_mid,
    adapter_down,
    adapter_up,
    tenant_counts,
    seg_starts,
    owner_slot,
):
    highest_precision_mode = lax.Precision.HIGHEST
    seq_count = lax.axis_size("seq")
    my_index = lax.axis_index("seq")
    shard_index = lax.axis_index(("tensor", "sub"))
    tok_rows, width_local = layer_input.shape
    ten_dev = adapter_down.shape[0]
    rank_width = adapter_down.shape[2]
    kv_local = adapter_up.shape[3]
    kv_total = out_grad.shape[2]
    blk_dev = tok_rows // BLK
    blocks = blk_dev * seq_count
    piece_cols = width_local // seq_count
    tenants = owner_slot.shape[0]
    tenant_ids = jnp.arange(tenants, dtype=jnp.int32)
    block_first, block_tenant, start_all, count_all, slot_all = tenant_tables(
        tenant_counts, seg_starts, owner_slot, blocks
    )
    my_first = lax.dynamic_slice_in_dim(block_first, my_index * blk_dev, blk_dev)
    my_start = lax.dynamic_slice_in_dim(start_all, my_index * blk_dev, blk_dev)
    my_count = lax.dynamic_slice_in_dim(count_all, my_index * blk_dev, blk_dev)
    my_slot = lax.dynamic_slice_in_dim(slot_all, my_index * blk_dev, blk_dev)
    offsets = my_first[:, None] + jnp.arange(BLK, dtype=jnp.int32)[None, :] - my_start[:, None]
    live_rows = offsets < my_count[:, None]
    masked = jnp.where(live_rows.reshape(tok_rows, 1, 1), out_grad, jnp.zeros_like(out_grad))
    masked_flat = masked.reshape(tok_rows, 2 * kv_total)
    masked_own = lax.dynamic_slice_in_dim(masked, shard_index * kv_local, kv_local, 2)
    gradient_block_list = masked_own.reshape(blk_dev, BLK, 2, kv_local)
    weight_full, up_all = (
        lax.all_gather(base_weight, "seq", axis=0, tiled=True),
        lax.all_gather(adapter_up, "seq", axis=0, tiled=True),
    )
    base_term = jnp.dot(masked_flat, weight_full, preferred_element_type=jnp.float32)
    own_select = (my_slot[:, None] == tenant_ids[None, :]).astype(jnp.bfloat16)
    up_projection_blocks = jnp.einsum(
        "bt,tjrk->bjrk", own_select, up_all, preferred_element_type=jnp.float32
    ).astype(jnp.bfloat16)
    low_part = jnp.einsum(
        "zpex,zehx->zpeh",
        gradient_block_list,
        up_projection_blocks,
        preferred_element_type=jnp.float32,
    ).reshape(tok_rows, rank_width)
    reduced_rank_sum = lax.psum(low_part, ("tensor", "sub"))
    reduced_rank_mine = (adapter_scale_factor * reduced_rank_sum).astype(jnp.bfloat16)
    lowrank_all = lax.all_gather(reduced_rank_mine, "seq", axis=0, tiled=True)
    mid_blocks = adapter_mid.reshape(blk_dev, BLK, 2, rank_width // 2)
    up_projection_share = adapter_scale_factor * jnp.einsum(
        "bqjr,bqjk->bjrk", mid_blocks, gradient_block_list, preferred_element_type=jnp.float32
    )
    block_select = (my_slot[:, None] == tenant_ids[None, :]).astype(jnp.float32)
    up_grad = lax.psum_scatter(
        jnp.einsum(
            "on,olqp->nlqp", block_select, up_projection_share, precision=highest_precision_mode
        ),
        "seq",
        scatter_dimension=0,
        tiled=True,
    )
    up_adapter_gradient = up_grad.astype(jnp.bfloat16)
    input_cols = layer_input.reshape(tok_rows, seq_count, piece_cols)
    down_cols = adapter_down.reshape(ten_dev, seq_count, piece_cols, rank_width)
    feat_rows, down_feat = (
        lax.all_to_all(input_cols, "seq", split_axis=1, concat_axis=0, tiled=True),
        lax.all_to_all(down_cols, "seq", split_axis=1, concat_axis=0, tiled=True),
    )
    feat_blocks = feat_rows.reshape(blocks, BLK, piece_cols)
    down_feat = down_feat.reshape(tenants, piece_cols, rank_width)
    low_blocks = lowrank_all.reshape(blocks, BLK, rank_width)
    adapter_slot_choice = slot_all[:, None] == tenant_ids[None, :]
    down_projection_share = jnp.einsum(
        "bqc,bqr->bcr", feat_blocks, low_blocks, preferred_element_type=jnp.float32
    )
    down_grad = jnp.einsum(
        "bt,bcr->tcr",
        adapter_slot_choice.astype(jnp.float32),
        down_projection_share,
        precision=highest_precision_mode,
    ).astype(jnp.bfloat16)
    down_projection_blocks = jnp.einsum(
        "bt,tcr->bcr",
        adapter_slot_choice.astype(jnp.bfloat16),
        down_feat,
        preferred_element_type=jnp.float32,
    ).astype(jnp.bfloat16)
    side_feat = jnp.einsum(
        "bqr,bcr->bqc", low_blocks, down_projection_blocks, preferred_element_type=jnp.float32
    ).astype(jnp.bfloat16)
    grad_down, adapter_side_term = (
        lax.all_to_all(
            down_grad.reshape(seq_count, ten_dev, piece_cols, rank_width),
            "seq",
            split_axis=0,
            concat_axis=2,
            tiled=True,
        ),
        lax.all_to_all(
            side_feat.reshape(seq_count, tok_rows, piece_cols),
            "seq",
            split_axis=0,
            concat_axis=2,
            tiled=True,
        ),
    )
    grad_input = (
        base_term + adapter_side_term.reshape(tok_rows, width_local).astype(jnp.float32)
    ).astype(jnp.bfloat16)
    return (grad_input, grad_down.reshape(ten_dev, width_local, rank_width), up_adapter_gradient)


MESH = pl.DeviceIdType.MESH
CHUNKS = 2
F32 = jnp.float32
BF16 = jnp.bfloat16


def hosting(planes, tok_blocks):
    blocks, tenants = planes * tok_blocks, planes * 2
    low, high = [], []
    for s in range(planes):
        first, last = s * tok_blocks, (s + 1) * tok_blocks - 1
        least = max(first // tok_blocks, first - (blocks - tenants))
        most = min(last, tenants - 1 - (blocks - 1 - last) // tok_blocks)
        if least < planes:
            low.append(s)
        if most >= planes:
            high.append(s)
    return max(low), min(high)


def line_kernel(
    S, T, C,
    counts, starts, owners,
    x, og, mid, w_hbm, dn_hbm, up_hbm,
    gi, gd, gu,
    w, dn, up, low, gown, gright, gleft, uown, uright, uleft, masked, lsel, msel,
    copy_sem, up_s, up_r, low_s, low_r,
    w_s, w_r, y_s, y_r, dn_s, dn_r, g_s, g_r, u_s, u_r,
):
    s = lax.axis_index("seq")
    g = lax.axis_index("groups")
    t = lax.axis_index("tensor")
    c = lax.axis_index("sub")
    M = T * C
    m = t * C + c
    rows, width = x.shape
    depth = w_hbm.shape[0]
    half = depth // 2
    piece = half // CHUNKS
    kv_local = up_hbm.shape[3]
    kv = kv_local * M
    nblk = rows // BLK
    N = 2 * S
    rank2 = mid.shape[1]
    rank = rank2 // 2
    last0, first1 = hosting(S, nblk)
    right, left = {"seq": s + 1}, {"seq": s - 1}

    def partners():
        for k in range(1, M):
            q = lax.rem(m + k, M)
            yield k, {"tensor": q // C, "sub": lax.rem(q, C)}

    def remote(src, dst, send, recv, dev):
        return pltpu.make_async_remote_copy(
            src_ref=src, dst_ref=dst, send_sem=send, recv_sem=recv, device_id=dev, device_id_type=MESH
        )

    own = (
        pltpu.make_async_copy(w_hbm, w.at[pl.ds(s * depth, depth)], copy_sem.at[0]),
        pltpu.make_async_copy(dn_hbm, dn.at[pl.ds(2 * s, 2)], copy_sem.at[1]),
        pltpu.make_async_copy(up_hbm, up.at[pl.ds(2 * s, 2)], copy_sem.at[2]),
    )
    for cp in own:
        cp.start()

    barrier = pltpu.get_barrier_semaphore()
    for k in range(1, S):
        pl.semaphore_signal(barrier, inc=1, device_id={"seq": lax.rem(s + k, S)}, device_id_type=MESH)
    pl.semaphore_signal(barrier, inc=1, device_id={"groups": 1 - g}, device_id_type=MESH)
    for _, dev in partners():
        pl.semaphore_signal(barrier, inc=1, device_id=dev, device_id_type=MESH)
    pl.semaphore_wait(barrier, S - 1 + 1 + M - 1)
    for cp in own:
        cp.wait()

    def up_copy(k, plane, target):
        part = up.at[pl.ds(2 * plane, 2)]
        return remote(part, part, up_s.at[k - 1], up_r.at[k - 1], {"seq": target})

    for k in range(1, S):
        up_copy(k, s, lax.rem(s + k, S)).start()

    def w_rows(plane, hlf, i):
        return w.at[pl.ds(pl.multiple_of(plane * depth + hlf * half + i * piece, 16), piece)]

    def origin(way, k):
        return s - k if way == 0 else s + k

    def held(plane):
        return jnp.logical_and(plane >= 0, plane < S)

    def w_copy(way, k, plane, i):
        part = w_rows(plane, g, i)
        return remote(part, part, w_s.at[way, k - 1, i], w_r.at[way, k - 1, i], left if way else right)

    def y_copy(way, k, plane, i, hlf):
        part = w_rows(plane, hlf, i)
        return remote(part, part, y_s.at[way, k - 1, i], y_r.at[way, k - 1, i], {"groups": 1 - g})

    def dn_copy(way, k, plane, j):
        part = dn.at[2 * plane + j]
        return remote(part, part, dn_s.at[way, k - 1, j], dn_r.at[way, k - 1, j], left if way else right)

    def can_send(way, k, j=None):
        plane = origin(way, k - 1)
        nxt = s - 1 if way else s + 1
        ok = jnp.logical_and(held(plane), held(nxt))
        if j == 0:
            ok = jnp.logical_and(ok, nxt <= last0)
        if j == 1:
            ok = jnp.logical_and(ok, nxt >= first1)
        return ok

    def can_recv(way, k, j=None):
        ok = held(origin(way, k))
        if j == 0:
            ok = jnp.logical_and(ok, s <= last0)
        if j == 1:
            ok = jnp.logical_and(ok, s >= first1)
        return ok

    def send_w(k, way, i):
        @pl.when(can_send(way, k))
        def _():
            w_copy(way, k, origin(way, k - 1), i).start()

    def send_dn(k, way, j):
        @pl.when(can_send(way, k, j))
        def _():
            dn_copy(way, k, origin(way, k - 1), j).start()

    for i in range(CHUNKS):
        for way in range(2):
            send_w(1, way, i)
    for j in range(2):
        for way in range(2):
            send_dn(1, way, j)

    for p in range(S):
        for j in range(2):
            unused = s > last0 if j == 0 else s < first1

            @pl.when(jnp.logical_and(unused, s != p))
            def _(p=p, j=j):
                dn[2 * p + j] = jnp.zeros(dn.shape[1:], dn.dtype)

    slots = []
    for b in range(nblk):
        first = (s * nblk + b) * BLK
        tenant = jnp.int32(-1)
        for n in range(N):
            tenant = tenant + jnp.where(starts[n] <= first, 1, 0).astype(jnp.int32)
        live = counts[tenant] - (first - starts[tenant])
        slots.append(owners[tenant])
        here = pl.ds(b * BLK, BLK)
        keep = lax.broadcasted_iota(jnp.int32, (BLK, 2 * kv), 0) < live
        value = og[here, :].astype(F32)
        masked[here, :] = jnp.where(keep, value, 0.0).astype(BF16)

    def own_features(j):
        return pl.ds(pl.multiple_of(j * kv + m * kv_local, 128), kv_local)

    for k in range(1, S):
        up_copy(k, lax.rem(s + S - k, S), s).wait_recv()
    for b in range(nblk):
        here = pl.ds(b * BLK, BLK)
        for j in range(2):
            low[m, here, j * rank : (j + 1) * rank] = lax.dot_general(
                masked[here, own_features(j)],
                up[slots[b], j],
                (((1,), (1,)), ((), ())),
                preferred_element_type=F32,
            )

    def low_copy(k, index, dev):
        return remote(low.at[index], low.at[index], low_s.at[k - 1], low_r.at[k - 1], dev)

    for k, dev in partners():
        low_copy(k, m, dev).start()

    for b in range(nblk):
        here = pl.ds(b * BLK, BLK)
        value = mid[here, :].astype(F32)
        for n in range(N):
            hit = jnp.where(slots[b] == n, 1.0, 0.0).astype(F32)
            msel[here, n * rank2 : (n + 1) * rank2] = (value * hit).astype(BF16)
    for n in range(N):
        both = msel[:, n * rank2 : (n + 1) * rank2]
        for j in range(2):
            share = lax.dot_general(
                both, masked[:, own_features(j)], (((0,), (0,)), ((), ())), preferred_element_type=F32
            )
            uown[n, j] = (adapter_scale_factor * share[j * rank : (j + 1) * rank, :]).astype(BF16)

    for k, dev in partners():
        low_copy(k, lax.rem(m + M - k, M), dev).wait_recv()
    total = low[0]
    for q in range(1, M):
        total = total + low[q]
    lowrank = (adapter_scale_factor * total).astype(BF16).astype(F32)
    for b in range(nblk):
        here = pl.ds(b * BLK, BLK)
        value = lowrank[b * BLK : (b + 1) * BLK, :]
        for n in range(N):
            hit = jnp.where(slots[b] == n, 1.0, 0.0).astype(F32)
            lsel[here, n * rank2 : (n + 1) * rank2] = (value * hit).astype(BF16)

    step = 256

    @pl.loop(0, width // step)
    def _(i):
        at = pl.ds(pl.multiple_of(i * step, step), step)
        share = lax.dot_general(
            x[:, at], lsel[...], (((0,), (0,)), ((), ())), preferred_element_type=F32
        )
        for n in range(N):
            gown[n, at, :] = share[:, n * rank2 : (n + 1) * rank2].astype(BF16)

    g_in, u_in = (gright, gleft), (uright, uleft)

    def grad_copies(way, d, j):
        n = 2 * d + j
        dev = left if way else right
        return (
            remote(gown.at[n], g_in[way].at[n], g_s.at[n], g_r.at[way, n], dev),
            remote(uown.at[n], u_in[way].at[n], u_s.at[n], u_r.at[way, n], dev),
        )

    def gives(way, plane, j):
        if way == 0:
            return plane >= (0 if j == 0 else first1)
        return plane <= (last0 if j == 0 else S - 1)

    def add_in(way, n):
        @pl.loop(0, width // step)
        def _(i):
            at = pl.ds(pl.multiple_of(i * step, step), step)
            gown[n, at, :] = (gown[n, at, :].astype(F32) + g_in[way][n, at, :].astype(F32)).astype(BF16)

        uown[n] = (uown[n].astype(F32) + u_in[way][n].astype(F32)).astype(BF16)

    def grad_step(way, plane):
        @pl.when(s == plane)
        def _():
            behind = plane + 1 if way else plane - 1
            dests = range(plane, -1, -1) if way else range(plane, S)
            for d in reversed(dests):
                for j in range(2):
                    if 0 <= behind < S and gives(way, behind, j):
                        for cp in grad_copies(way, d, j):
                            cp.wait_recv()
                        add_in(way, 2 * d + j)
                    if d != plane and gives(way, plane, j):
                        for cp in grad_copies(way, d, j):
                            cp.start()

    grad_step(0, 0)
    grad_step(1, S - 1)
    for k in range(1, S):
        for i in range(CHUNKS):
            for way in range(2):

                @pl.when(can_recv(way, k))
                def _(way=way, i=i):
                    w_copy(way, k, origin(way, k), i).wait_recv()
                    y_copy(way, k, origin(way, k), i, g).start()

                if k < S - 1:
                    send_w(k + 1, way, i)
        for j in range(2):
            for way in range(2):

                @pl.when(can_recv(way, k, j))
                def _(way=way, j=j):
                    dn_copy(way, k, origin(way, k), j).wait_recv()

                if k < S - 1:
                    send_dn(k + 1, way, j)
        grad_step(0, k)
        grad_step(1, S - 1 - k)

    gd[...] = gown[pl.ds(2 * s, 2)]
    gu[...] = uown[pl.ds(2 * s, 2)]

    for k in range(1, S):
        for i in range(CHUNKS):
            for way in range(2):

                @pl.when(can_recv(way, k))
                def _(way=way, i=i, k=k):
                    y_copy(way, k, origin(way, k), i, 1 - g).wait_recv()

    @pl.loop(0, width // step)
    def _(i):
        at = pl.ds(pl.multiple_of(i * step, step), step)
        base = jnp.dot(masked[...], w[:, at], preferred_element_type=F32)
        side = jnp.zeros((rows, step), F32)
        for n in range(N):
            side = side + lax.dot_general(
                lsel[:, n * rank2 : (n + 1) * rank2],
                dn[n, at, :],
                (((1,), (1,)), ((), ())),
                preferred_element_type=F32,
            )
        gi[:, at] = (base + side.astype(BF16).astype(F32)).astype(BF16)

    for k in range(1, S):
        up_copy(k, s, lax.rem(s + k, S)).wait_send()
    for k, dev in partners():
        low_copy(k, m, dev).wait_send()
    for k in range(1, S):
        for way in range(2):
            for i in range(CHUNKS):

                @pl.when(can_send(way, k))
                def _(k=k, way=way, i=i):
                    w_copy(way, k, origin(way, k - 1), i).wait_send()

                @pl.when(can_recv(way, k))
                def _(k=k, way=way, i=i):
                    y_copy(way, k, origin(way, k), i, g).wait_send()

            for j in range(2):

                @pl.when(can_send(way, k, j))
                def _(k=k, way=way, j=j):
                    dn_copy(way, k, origin(way, k - 1), j).wait_send()

    for plane in range(S):

        @pl.when(s == plane)
        def _(plane=plane):
            for d in range(S):
                for j in range(2):
                    way = 0 if d > plane else 1
                    if d != plane and gives(way, plane, j):
                        for cp in grad_copies(way, d, j):
                            cp.wait_send()


def line_local(S, T, C, layer_input, out_grad, base_weight, adapter_mid, adapter_down, adapter_up,
               tenant_counts, seg_starts, owner_slot):
    rows, width = layer_input.shape
    N, M = 2 * S, T * C
    rank2 = adapter_down.shape[2]
    kv2 = 2 * out_grad.shape[2]
    up_shape = adapter_up.shape[1:]
    vmem = pl.BlockSpec(memory_space=pltpu.VMEM)
    smem = pl.BlockSpec(memory_space=pltpu.SMEM)
    hbm = pl.BlockSpec(memory_space=pl.ANY)
    dma = pltpu.SemaphoreType.DMA
    grads = pltpu.VMEM((N, width, rank2), BF16)
    ups = pltpu.VMEM((N,) + up_shape, BF16)
    return pl.pallas_call(
        functools.partial(line_kernel, S, T, C),
        out_shape=(
            jax.ShapeDtypeStruct((rows, width), BF16),
            jax.ShapeDtypeStruct(adapter_down.shape, BF16),
            jax.ShapeDtypeStruct(adapter_up.shape, BF16),
        ),
        in_specs=[smem] * 3 + [vmem] * 3 + [hbm] * 3,
        out_specs=(vmem, vmem, vmem),
        scratch_shapes=[
            pltpu.VMEM((S * base_weight.shape[0], width), BF16),
            grads,
            ups,
            pltpu.VMEM((M, rows, rank2), F32),
            grads, grads, grads,
            ups, ups, ups,
            pltpu.VMEM((rows, kv2), BF16),
            pltpu.VMEM((rows, N * rank2), BF16),
            pltpu.VMEM((rows, N * rank2), BF16),
            dma((3,)),
            dma((S - 1,)), dma((S - 1,)),
            dma((M - 1,)), dma((M - 1,)),
            dma((2, S - 1, CHUNKS)), dma((2, S - 1, CHUNKS)),
            dma((2, S - 1, CHUNKS)), dma((2, S - 1, CHUNKS)),
            dma((2, S - 1, 2)), dma((2, S - 1, 2)),
            dma((N,)), dma((2, N)),
            dma((N,)), dma((2, N)),
        ],
        compiler_params=pltpu.CompilerParams(
            collective_id=0, has_side_effects=True, vmem_limit_bytes=58 * 1024 * 1024
        ),
        name="line",
    )(
        tenant_counts, seg_starts, owner_slot,
        layer_input, out_grad.reshape(rows, kv2), adapter_mid, base_weight, adapter_down, adapter_up,
    )


def solution(mesh):
    S, T, C = mesh.shape["seq"], mesh.shape["tensor"], mesh.shape["sub"]
    short = 2 <= S <= 4 and mesh.shape["groups"] == 2
    body = functools.partial(line_local, S, T, C) if short else local

    return jax.shard_map(
        body,
        mesh=mesh,
        in_specs=(
            P(("groups", "seq"), ("tensor", "sub")),
            P(("groups", "seq"), None, None),
            P("seq", ("tensor", "sub")),
            P(("groups", "seq"), None),
            P(("groups", "seq"), ("tensor", "sub"), None),
            P(("groups", "seq"), None, None, ("tensor", "sub")),
            P("groups"),
            P("groups"),
            P("groups"),
        ),
        out_specs=(
            P(("groups", "seq"), ("tensor", "sub")),
            P(("groups", "seq"), ("tensor", "sub"), None),
            P(("groups", "seq"), None, None, ("tensor", "sub")),
        ),
        check_vma=False,
    )
```

```python
import functools

import jax
import jax.numpy as jnp
from jax import lax
from jax.experimental import pallas as pl
from jax.experimental.pallas import tpu as pltpu
from jax.sharding import PartitionSpec as P

BLK = 128


adapter_scale_factor = 2.0


def tenant_tables(tenant_counts, seg_starts, owner_slot, blocks):
    tenant_ids = jnp.arange(owner_slot.shape[0], dtype=jnp.int32)
    block_first = jnp.arange(blocks, dtype=jnp.int32) * BLK
    block_tenant = (
        jnp.sum((seg_starts[None, :] <= block_first[:, None]).astype(jnp.int32), axis=1) - 1
    )
    tenant_hit = block_tenant[:, None] == tenant_ids[None, :]

    def per_block(values):
        return jnp.sum(jnp.where(tenant_hit, values[None, :], 0), axis=1)

    return (
        block_first,
        block_tenant,
        per_block(seg_starts),
        per_block(tenant_counts),
        per_block(owner_slot),
    )


def local(
    layer_input,
    out_grad,
    base_weight,
    adapter_mid,
    adapter_down,
    adapter_up,
    tenant_counts,
    seg_starts,
    owner_slot,
):
    highest_precision_mode = lax.Precision.HIGHEST
    seq_count = lax.axis_size("seq")
    my_index = lax.axis_index("seq")
    shard_index = lax.axis_index(("tensor", "sub"))
    tok_rows, width_local = layer_input.shape
    ten_dev = adapter_down.shape[0]
    rank_width = adapter_down.shape[2]
    kv_local = adapter_up.shape[3]
    kv_total = out_grad.shape[2]
    blk_dev = tok_rows // BLK
    blocks = blk_dev * seq_count
    piece_cols = width_local // seq_count
    tenants = owner_slot.shape[0]
    tenant_ids = jnp.arange(tenants, dtype=jnp.int32)
    block_first, block_tenant, start_all, count_all, slot_all = tenant_tables(
        tenant_counts, seg_starts, owner_slot, blocks
    )
    my_first = lax.dynamic_slice_in_dim(block_first, my_index * blk_dev, blk_dev)
    my_start = lax.dynamic_slice_in_dim(start_all, my_index * blk_dev, blk_dev)
    my_count = lax.dynamic_slice_in_dim(count_all, my_index * blk_dev, blk_dev)
    my_slot = lax.dynamic_slice_in_dim(slot_all, my_index * blk_dev, blk_dev)
    offsets = my_first[:, None] + jnp.arange(BLK, dtype=jnp.int32)[None, :] - my_start[:, None]
    live_rows = offsets < my_count[:, None]
    masked = jnp.where(live_rows.reshape(tok_rows, 1, 1), out_grad, jnp.zeros_like(out_grad))
    masked_flat = masked.reshape(tok_rows, 2 * kv_total)
    masked_own = lax.dynamic_slice_in_dim(masked, shard_index * kv_local, kv_local, 2)
    gradient_block_list = masked_own.reshape(blk_dev, BLK, 2, kv_local)
    weight_full, up_all = (
        lax.all_gather(base_weight, "seq", axis=0, tiled=True),
        lax.all_gather(adapter_up, "seq", axis=0, tiled=True),
    )
    base_term = jnp.dot(masked_flat, weight_full, preferred_element_type=jnp.float32)
    own_select = (my_slot[:, None] == tenant_ids[None, :]).astype(jnp.bfloat16)
    up_projection_blocks = jnp.einsum(
        "bt,tjrk->bjrk", own_select, up_all, preferred_element_type=jnp.float32
    ).astype(jnp.bfloat16)
    low_part = jnp.einsum(
        "zpex,zehx->zpeh",
        gradient_block_list,
        up_projection_blocks,
        preferred_element_type=jnp.float32,
    ).reshape(tok_rows, rank_width)
    reduced_rank_sum = lax.psum(low_part, ("tensor", "sub"))
    reduced_rank_mine = (adapter_scale_factor * reduced_rank_sum).astype(jnp.bfloat16)
    lowrank_all = lax.all_gather(reduced_rank_mine, "seq", axis=0, tiled=True)
    mid_blocks = adapter_mid.reshape(blk_dev, BLK, 2, rank_width // 2)
    up_projection_share = adapter_scale_factor * jnp.einsum(
        "bqjr,bqjk->bjrk", mid_blocks, gradient_block_list, preferred_element_type=jnp.float32
    )
    block_select = (my_slot[:, None] == tenant_ids[None, :]).astype(jnp.float32)
    up_grad = lax.psum_scatter(
        jnp.einsum(
            "on,olqp->nlqp", block_select, up_projection_share, precision=highest_precision_mode
        ),
        "seq",
        scatter_dimension=0,
        tiled=True,
    )
    up_adapter_gradient = up_grad.astype(jnp.bfloat16)
    input_cols = layer_input.reshape(tok_rows, seq_count, piece_cols)
    down_cols = adapter_down.reshape(ten_dev, seq_count, piece_cols, rank_width)
    feat_rows, down_feat = (
        lax.all_to_all(input_cols, "seq", split_axis=1, concat_axis=0, tiled=True),
        lax.all_to_all(down_cols, "seq", split_axis=1, concat_axis=0, tiled=True),
    )
    feat_blocks = feat_rows.reshape(blocks, BLK, piece_cols)
    down_feat = down_feat.reshape(tenants, piece_cols, rank_width)
    low_blocks = lowrank_all.reshape(blocks, BLK, rank_width)
    adapter_slot_choice = slot_all[:, None] == tenant_ids[None, :]
    down_projection_share = jnp.einsum(
        "bqc,bqr->bcr", feat_blocks, low_blocks, preferred_element_type=jnp.float32
    )
    down_grad = jnp.einsum(
        "bt,bcr->tcr",
        adapter_slot_choice.astype(jnp.float32),
        down_projection_share,
        precision=highest_precision_mode,
    ).astype(jnp.bfloat16)
    down_projection_blocks = jnp.einsum(
        "bt,tcr->bcr",
        adapter_slot_choice.astype(jnp.bfloat16),
        down_feat,
        preferred_element_type=jnp.float32,
    ).astype(jnp.bfloat16)
    side_feat = jnp.einsum(
        "bqr,bcr->bqc", low_blocks, down_projection_blocks, preferred_element_type=jnp.float32
    ).astype(jnp.bfloat16)
    grad_down, adapter_side_term = (
        lax.all_to_all(
            down_grad.reshape(seq_count, ten_dev, piece_cols, rank_width),
            "seq",
            split_axis=0,
            concat_axis=2,
            tiled=True,
        ),
        lax.all_to_all(
            side_feat.reshape(seq_count, tok_rows, piece_cols),
            "seq",
            split_axis=0,
            concat_axis=2,
            tiled=True,
        ),
    )
    grad_input = (
        base_term + adapter_side_term.reshape(tok_rows, width_local).astype(jnp.float32)
    ).astype(jnp.bfloat16)
    return (grad_input, grad_down.reshape(ten_dev, width_local, rank_width), up_adapter_gradient)


MESH = pl.DeviceIdType.MESH
CHUNKS = 2
F32 = jnp.float32
BF16 = jnp.bfloat16


def hosting(planes, tok_blocks):
    blocks, tenants = planes * tok_blocks, planes * 2
    low, high = [], []
    for s in range(planes):
        first, last = s * tok_blocks, (s + 1) * tok_blocks - 1
        least = max(first // tok_blocks, first - (blocks - tenants))
        most = min(last, tenants - 1 - (blocks - 1 - last) // tok_blocks)
        if least < planes:
            low.append(s)
        if most >= planes:
            high.append(s)
    return max(low), min(high)


def line_kernel(
    S, T, C,
    counts, starts, owners,
    x, og, mid, w_hbm, dn_hbm, up_hbm,
    gi, gd, gu,
    w, dn, up, low, gown, gright, gleft, mix, uown, uright, uleft, masked, lsel, msel,
    copy_sem, up_s, up_r, low_s, low_r,
    w_s, w_r, y_s, y_r, dn_s, dn_r, g_s, g_r, u_s, u_r,
):
    s = lax.axis_index("seq")
    g = lax.axis_index("groups")
    t = lax.axis_index("tensor")
    c = lax.axis_index("sub")
    M = T * C
    m = t * C + c
    rows, width = x.shape
    depth = w_hbm.shape[0]
    half = depth // 2
    piece = half // CHUNKS
    kv_local = up_hbm.shape[3]
    kv = kv_local * M
    nblk = rows // BLK
    N = 2 * S
    rank2 = mid.shape[1]
    rank = rank2 // 2
    last0, first1 = hosting(S, nblk)
    right, left = {"seq": s + 1}, {"seq": s - 1}

    def stage(axis):
        size, index = (C, c) if axis == "sub" else (T, t)
        for k in range(1, size):
            yield k, {axis: lax.rem(index + k, size)}, lax.rem(index + size - k, size)

    def remote(src, dst, send, recv, dev):
        return pltpu.make_async_remote_copy(
            src_ref=src, dst_ref=dst, send_sem=send, recv_sem=recv, device_id=dev, device_id_type=MESH
        )

    own = (
        pltpu.make_async_copy(w_hbm, w.at[pl.ds(s * depth, depth)], copy_sem.at[0]),
        pltpu.make_async_copy(dn_hbm, dn.at[pl.ds(2 * s, 2)], copy_sem.at[1]),
        pltpu.make_async_copy(up_hbm, up.at[pl.ds(2 * s, 2)], copy_sem.at[2]),
    )
    for cp in own:
        cp.start()

    barrier = pltpu.get_barrier_semaphore()
    for k in range(1, S):
        pl.semaphore_signal(barrier, inc=1, device_id={"seq": lax.rem(s + k, S)}, device_id_type=MESH)
    pl.semaphore_signal(barrier, inc=1, device_id={"groups": 1 - g}, device_id_type=MESH)
    for axis in ("sub", "tensor"):
        for _, dev, _ in stage(axis):
            pl.semaphore_signal(barrier, inc=1, device_id=dev, device_id_type=MESH)
    pl.semaphore_wait(barrier, S - 1 + 1 + C - 1 + T - 1)
    for cp in own:
        cp.wait()

    def up_copy(k, plane, target, j):
        part = up.at[2 * plane + j]
        return remote(part, part, up_s.at[k - 1, j], up_r.at[k - 1, j], {"seq": target})

    def wants(plane, j):
        return plane <= last0 if j == 0 else plane >= first1

    def ups(act):
        for k in range(1, S):
            for j in range(2):
                ahead, behind = lax.rem(s + k, S), lax.rem(s + S - k, S)
                if act == "recv":

                    @pl.when(wants(s, j))
                    def _(k=k, j=j, behind=behind):
                        up_copy(k, behind, s, j).wait_recv()

                else:

                    @pl.when(wants(ahead, j))
                    def _(k=k, j=j, ahead=ahead):
                        cp = up_copy(k, s, ahead, j)
                        cp.start() if act == "start" else cp.wait_send()

    ups("start")

    def w_rows(plane, hlf, i):
        return w.at[pl.ds(pl.multiple_of(plane * depth + hlf * half + i * piece, 16), piece)]

    def origin(way, k):
        return s - k if way == 0 else s + k

    def held(plane):
        return jnp.logical_and(plane >= 0, plane < S)

    def w_copy(way, k, plane, i):
        part = w_rows(plane, g, i)
        return remote(part, part, w_s.at[way, k - 1, i], w_r.at[way, k - 1, i], left if way else right)

    def y_copy(way, k, plane, i, hlf):
        part = w_rows(plane, hlf, i)
        return remote(part, part, y_s.at[way, k - 1, i], y_r.at[way, k - 1, i], {"groups": 1 - g})

    def dn_copy(way, k, plane, j):
        part = dn.at[2 * plane + j]
        return remote(part, part, dn_s.at[way, k - 1, j], dn_r.at[way, k - 1, j], left if way else right)

    def can_send(way, k, j=None):
        plane = origin(way, k - 1)
        nxt = s - 1 if way else s + 1
        ok = jnp.logical_and(held(plane), held(nxt))
        if j == 0:
            ok = jnp.logical_and(ok, nxt <= last0)
        if j == 1:
            ok = jnp.logical_and(ok, nxt >= first1)
        return ok

    def can_recv(way, k, j=None):
        ok = held(origin(way, k))
        if j == 0:
            ok = jnp.logical_and(ok, s <= last0)
        if j == 1:
            ok = jnp.logical_and(ok, s >= first1)
        return ok

    def send_w(k, way, i):
        @pl.when(can_send(way, k))
        def _():
            w_copy(way, k, origin(way, k - 1), i).start()

    cut = (S // 2 - 1, S // 2)

    def tenant_of(block):
        index = jnp.int32(-1)
        for n in range(N):
            index = index + jnp.where(starts[n] <= block * BLK, 1, 0).astype(jnp.int32)
        return index

    takes_grads = (tenant_of(S // 2 * nblk - 1) >= S, tenant_of(S // 2 * nblk) < S)

    def mix_copy(k, way):
        to = dn.at[2 * origin(way, k - 1) + way]
        dev = left if way else right
        return remote(mix.at[way, k - 1], to, dn_s.at[way, k - 1, way], dn_r.at[way, k - 1, way], dev)

    def dn_sends(k, way, j, act):
        ok = can_send(way, k, j)
        if j == way:

            @pl.when(jnp.logical_and(ok, s == cut[way]))
            def _():
                if act == "wait":
                    mix_copy(k, way).wait_send()

            ok = jnp.logical_and(ok, s != cut[way])

        @pl.when(ok)
        def _():
            cp = dn_copy(way, k, origin(way, k - 1), j)
            cp.wait_send() if act == "wait" else cp.start()

    def send_dn(k, way, j):
        dn_sends(k, way, j, "start")

    def mixed_dest(way, k):
        return k - 1 if way else S - k

    def mixed(way, plane, j):
        return plane == cut[way] and j != way

    def send_mix(k, way):
        @pl.when(s == cut[way])
        def _():
            hit = jnp.where(takes_grads[way], 1.0, 0.0).astype(F32)
            own_map = 2 * origin(way, k - 1) + way
            n = 2 * mixed_dest(way, k) + 1 - way

            @pl.loop(0, width // 256)
            def _(i):
                at = pl.ds(pl.multiple_of(i * 256, 256), 256)
                value = gown[n, at, :].astype(F32) * hit + dn[own_map, at, :].astype(F32) * (1.0 - hit)
                mix[way, k - 1, at, :] = value.astype(BF16)

            mix_copy(k, way).start()

    for i in range(CHUNKS):
        for way in range(2):
            send_w(1, way, i)
    for j in range(2):
        for way in range(2):
            send_dn(1, way, j)

    for p in range(S):
        for j in range(2):
            unused = s > last0 if j == 0 else s < first1

            @pl.when(jnp.logical_and(unused, s != p))
            def _(p=p, j=j):
                dn[2 * p + j] = jnp.zeros(dn.shape[1:], dn.dtype)

    slots = []
    for b in range(nblk):
        first = (s * nblk + b) * BLK
        tenant = jnp.int32(-1)
        for n in range(N):
            tenant = tenant + jnp.where(starts[n] <= first, 1, 0).astype(jnp.int32)
        live = counts[tenant] - (first - starts[tenant])
        slots.append(owners[tenant])
        here = pl.ds(b * BLK, BLK)
        keep = lax.broadcasted_iota(jnp.int32, (BLK, kv), 0) < live
        for j in range(2):
            value = og[here, j, :].astype(F32)
            masked[here, j * kv : (j + 1) * kv] = jnp.where(keep, value, 0.0).astype(BF16)

    def own_features(j):
        return pl.ds(pl.multiple_of(j * kv + m * kv_local, 128), kv_local)

    ups("recv")
    for b in range(nblk):
        here = pl.ds(b * BLK, BLK)
        for j in range(2):
            low[c, here, j * rank : (j + 1) * rank] = lax.dot_general(
                masked[here, own_features(j)],
                up[slots[b], j],
                (((1,), (1,)), ((), ())),
                preferred_element_type=F32,
            )

    def low_copy(k, index, dev, first):
        return remote(
            low.at[first + index], low.at[first + index], low_s.at[first + k - 1], low_r.at[first + k - 1], dev
        )

    for k, dev, _ in stage("sub"):
        low_copy(k, c, dev, 0).start()
    for k, dev, behind in stage("sub"):
        low_copy(k, behind, dev, 0).wait_recv()
    chip_sum = low[0]
    for q in range(1, C):
        chip_sum = chip_sum + low[q]
    low[C + t] = chip_sum
    for k, dev, _ in stage("tensor"):
        low_copy(k, t, dev, C).start()

    for b in range(nblk):
        here = pl.ds(b * BLK, BLK)
        value = mid[here, :].astype(F32)
        for n in range(N):
            hit = jnp.where(slots[b] == n, 1.0, 0.0).astype(F32)
            msel[here, n * rank2 : (n + 1) * rank2] = (value * hit).astype(BF16)
    for n in range(N):
        both = msel[:, n * rank2 : (n + 1) * rank2]
        for j in range(2):
            share = lax.dot_general(
                both, masked[:, own_features(j)], (((0,), (0,)), ((), ())), preferred_element_type=F32
            )
            uown[n, j] = (adapter_scale_factor * share[j * rank : (j + 1) * rank, :]).astype(BF16)

    for k, dev, behind in stage("tensor"):
        low_copy(k, behind, dev, C).wait_recv()
    total = low[C]
    for q in range(1, T):
        total = total + low[C + q]
    lowrank = (adapter_scale_factor * total).astype(BF16).astype(F32)
    for b in range(nblk):
        here = pl.ds(b * BLK, BLK)
        value = lowrank[b * BLK : (b + 1) * BLK, :]
        for n in range(N):
            hit = jnp.where(slots[b] == n, 1.0, 0.0).astype(F32)
            lsel[here, n * rank2 : (n + 1) * rank2] = (value * hit).astype(BF16)

    def hop_w(k):
        for i in range(CHUNKS):
            for way in range(2):

                @pl.when(can_recv(way, k))
                def _(way=way, i=i):
                    w_copy(way, k, origin(way, k), i).wait_recv()
                    if k < S - 1:
                        send_w(k + 1, way, i)
                    y_copy(way, k, origin(way, k), i, g).start()

    def hop_dn(k):
        for j in range(2):
            for way in range(2):

                @pl.when(can_recv(way, k, j))
                def _(way=way, j=j):
                    dn_copy(way, k, origin(way, k), j).wait_recv()
                    if k < S - 1:
                        send_dn(k + 1, way, j)

                if j == way and k < S // 2:
                    send_mix(k + 1, way)

    def hop(k):
        hop_w(k)
        hop_dn(k)

    hop_w(1)
    step = 256

    @pl.loop(0, width // step)
    def _(i):
        at = pl.ds(pl.multiple_of(i * step, step), step)
        share = lax.dot_general(
            x[:, at], lsel[...], (((0,), (0,)), ((), ())), preferred_element_type=F32
        )
        for n in range(N):
            gown[n, at, :] = share[:, n * rank2 : (n + 1) * rank2].astype(BF16)

    g_in, u_in = (gright, gleft), (uright, uleft)

    def grad_copies(way, sender, d, j):
        n = 2 * d + j
        dev = left if way else right
        small = remote(uown.at[n], u_in[way].at[n], u_s.at[n], u_r.at[way, n], dev)
        if mixed(way, sender, j):
            return (small,)
        return (remote(gown.at[n], g_in[way].at[n], g_s.at[n], g_r.at[way, n], dev), small)

    def gives(way, plane, j):
        if way == 0:
            return plane >= (0 if j == 0 else first1)
        return plane <= (last0 if j == 0 else S - 1)

    def add_in(way, sender, d, j):
        n = 2 * d + j
        came, scale = g_in[way].at[n], None
        if mixed(way, sender, j):
            k = d + 1 if way else S - d
            came = dn.at[2 * (sender + k - 1 if way else sender - k + 1) + way]
            scale = jnp.where(takes_grads[way], 1.0, 0.0).astype(F32)

        @pl.loop(0, width // step)
        def _(i):
            at = pl.ds(pl.multiple_of(i * step, step), step)
            value = came[at, :].astype(F32)
            if scale is not None:
                value = value * scale
            gown[n, at, :] = (gown[n, at, :].astype(F32) + value).astype(BF16)

        uown[n] = (uown[n].astype(F32) + u_in[way][n].astype(F32)).astype(BF16)

    def grad_turn(way, plane, alone):
        @pl.when(s == plane)
        def _():
            behind = plane + 1 if way else plane - 1
            dests = range(plane - 1, -1, -1) if way else range(plane + 1, S)
            for d in reversed(dests):
                for j in range(2):
                    joined = 0 <= behind < S and gives(way, behind, j)
                    if joined != alone and gives(way, plane, j):
                        if joined:
                            for cp in grad_copies(way, behind, d, j):
                                cp.wait_recv()
                            add_in(way, behind, d, j)
                        for cp in grad_copies(way, plane, d, j):
                            cp.start()

    def grad_end(plane):
        @pl.when(s == plane)
        def _():
            for way in range(2):
                behind = plane + 1 if way else plane - 1
                for j in range(2):
                    if 0 <= behind < S and gives(way, behind, j):
                        for cp in grad_copies(way, behind, plane, j):
                            cp.wait_recv()
                        add_in(way, behind, plane, j)

    for way in range(2):
        send_mix(1, way)
    grad_turn(0, 0, True)
    grad_turn(1, S - 1, True)
    hop_dn(1)
    for p in range(1, S - 1):
        grad_turn(0, p, True)
        grad_turn(1, S - 1 - p, True)
    for k in range(2, S - 1):
        hop(k)
    for p in range(1, S - 1):
        grad_turn(0, p, False)
        grad_turn(1, S - 1 - p, False)
    if S > 2:
        hop(S - 1)

    for k in range(1, S):
        for i in range(CHUNKS):
            for way in range(2):

                @pl.when(can_recv(way, k))
                def _(way=way, i=i, k=k):
                    y_copy(way, k, origin(way, k), i, 1 - g).wait_recv()

    @pl.loop(0, width // step)
    def _(i):
        at = pl.ds(pl.multiple_of(i * step, step), step)
        base = jnp.dot(masked[...], w[:, at], preferred_element_type=F32)
        side = jnp.zeros((rows, step), F32)
        for n in range(N):
            side = side + lax.dot_general(
                lsel[:, n * rank2 : (n + 1) * rank2],
                dn[n, at, :],
                (((1,), (1,)), ((), ())),
                preferred_element_type=F32,
            )
        gi[:, at] = (base + side.astype(BF16).astype(F32)).astype(BF16)

    for p in range(S):
        grad_end(p)
    gd[...] = gown[pl.ds(2 * s, 2)]
    gu[...] = uown[pl.ds(2 * s, 2)]

    ups("wait")
    for k, dev, _ in stage("sub"):
        low_copy(k, c, dev, 0).wait_send()
    for k, dev, _ in stage("tensor"):
        low_copy(k, t, dev, C).wait_send()
    for k in range(1, S):
        for way in range(2):
            for i in range(CHUNKS):

                @pl.when(can_send(way, k))
                def _(k=k, way=way, i=i):
                    w_copy(way, k, origin(way, k - 1), i).wait_send()

                @pl.when(can_recv(way, k))
                def _(k=k, way=way, i=i):
                    y_copy(way, k, origin(way, k), i, g).wait_send()

            for j in range(2):

                dn_sends(k, way, j, "wait")

    for plane in range(S):

        @pl.when(s == plane)
        def _(plane=plane):
            for d in range(S):
                for j in range(2):
                    way = 0 if d > plane else 1
                    if d != plane and gives(way, plane, j):
                        for cp in grad_copies(way, plane, d, j):
                            cp.wait_send()


def line_local(S, T, C, layer_input, out_grad, base_weight, adapter_mid, adapter_down, adapter_up,
               tenant_counts, seg_starts, owner_slot):
    rows, width = layer_input.shape
    N = 2 * S
    rank2 = adapter_down.shape[2]
    kv2 = 2 * out_grad.shape[2]
    up_shape = adapter_up.shape[1:]
    vmem = pl.BlockSpec(memory_space=pltpu.VMEM)
    smem = pl.BlockSpec(memory_space=pltpu.SMEM)
    hbm = pl.BlockSpec(memory_space=pl.ANY)
    dma = pltpu.SemaphoreType.DMA
    grads = pltpu.VMEM((N, width, rank2), BF16)
    ups = pltpu.VMEM((N,) + up_shape, BF16)
    return pl.pallas_call(
        functools.partial(line_kernel, S, T, C),
        out_shape=(
            jax.ShapeDtypeStruct((rows, width), BF16),
            jax.ShapeDtypeStruct(adapter_down.shape, BF16),
            jax.ShapeDtypeStruct(adapter_up.shape, BF16),
        ),
        in_specs=[smem] * 3 + [vmem] * 3 + [hbm] * 3,
        out_specs=(vmem, vmem, vmem),
        scratch_shapes=[
            pltpu.VMEM((S * base_weight.shape[0], width), BF16),
            grads,
            ups,
            pltpu.VMEM((C + T, rows, rank2), F32),
            grads, grads, grads,
            pltpu.VMEM((2, S // 2, width, rank2), BF16),
            ups, ups, ups,
            pltpu.VMEM((rows, kv2), BF16),
            pltpu.VMEM((rows, N * rank2), BF16),
            pltpu.VMEM((rows, N * rank2), BF16),
            dma((3,)),
            dma((S - 1, 2)), dma((S - 1, 2)),
            dma((C + T,)), dma((C + T,)),
            dma((2, S - 1, CHUNKS)), dma((2, S - 1, CHUNKS)),
            dma((2, S - 1, CHUNKS)), dma((2, S - 1, CHUNKS)),
            dma((2, S - 1, 2)), dma((2, S - 1, 2)),
            dma((N,)), dma((2, N)),
            dma((N,)), dma((2, N)),
        ],
        compiler_params=pltpu.CompilerParams(
            collective_id=0, has_side_effects=True, vmem_limit_bytes=58 * 1024 * 1024
        ),
        name="line",
    )(
        tenant_counts, seg_starts, owner_slot,
        layer_input, out_grad, adapter_mid, base_weight, adapter_down, adapter_up,
    )


def solution(mesh):
    S, T, C = mesh.shape["seq"], mesh.shape["tensor"], mesh.shape["sub"]
    short = S == 4 and mesh.shape["groups"] == 2
    body = functools.partial(line_local, S, T, C) if short else local

    return jax.shard_map(
        body,
        mesh=mesh,
        in_specs=(
            P(("groups", "seq"), ("tensor", "sub")),
            P(("groups", "seq"), None, None),
            P("seq", ("tensor", "sub")),
            P(("groups", "seq"), None),
            P(("groups", "seq"), ("tensor", "sub"), None),
            P(("groups", "seq"), None, None, ("tensor", "sub")),
            P("groups"),
            P("groups"),
            P("groups"),
        ),
        out_specs=(
            P(("groups", "seq"), ("tensor", "sub")),
            P(("groups", "seq"), ("tensor", "sub"), None),
            P(("groups", "seq"), None, None, ("tensor", "sub")),
        ),
        check_vma=False,
    )
```

```python
import functools

import jax
import jax.numpy as jnp
from jax import lax
from jax.experimental import pallas as pl
from jax.experimental.pallas import tpu as pltpu
from jax.sharding import PartitionSpec as P

BLK = 128


adapter_scale_factor = 2.0


def tenant_tables(tenant_counts, seg_starts, owner_slot, blocks):
    tenant_ids = jnp.arange(owner_slot.shape[0], dtype=jnp.int32)
    block_first = jnp.arange(blocks, dtype=jnp.int32) * BLK
    block_tenant = (
        jnp.sum((seg_starts[None, :] <= block_first[:, None]).astype(jnp.int32), axis=1) - 1
    )
    tenant_hit = block_tenant[:, None] == tenant_ids[None, :]

    def per_block(values):
        return jnp.sum(jnp.where(tenant_hit, values[None, :], 0), axis=1)

    return (
        block_first,
        block_tenant,
        per_block(seg_starts),
        per_block(tenant_counts),
        per_block(owner_slot),
    )


def local(
    layer_input,
    out_grad,
    base_weight,
    adapter_mid,
    adapter_down,
    adapter_up,
    tenant_counts,
    seg_starts,
    owner_slot,
):
    highest_precision_mode = lax.Precision.HIGHEST
    seq_count = lax.axis_size("seq")
    my_index = lax.axis_index("seq")
    shard_index = lax.axis_index(("tensor", "sub"))
    tok_rows, width_local = layer_input.shape
    ten_dev = adapter_down.shape[0]
    rank_width = adapter_down.shape[2]
    kv_local = adapter_up.shape[3]
    kv_total = out_grad.shape[2]
    blk_dev = tok_rows // BLK
    blocks = blk_dev * seq_count
    piece_cols = width_local // seq_count
    tenants = owner_slot.shape[0]
    tenant_ids = jnp.arange(tenants, dtype=jnp.int32)
    block_first, block_tenant, start_all, count_all, slot_all = tenant_tables(
        tenant_counts, seg_starts, owner_slot, blocks
    )
    my_first = lax.dynamic_slice_in_dim(block_first, my_index * blk_dev, blk_dev)
    my_start = lax.dynamic_slice_in_dim(start_all, my_index * blk_dev, blk_dev)
    my_count = lax.dynamic_slice_in_dim(count_all, my_index * blk_dev, blk_dev)
    my_slot = lax.dynamic_slice_in_dim(slot_all, my_index * blk_dev, blk_dev)
    offsets = my_first[:, None] + jnp.arange(BLK, dtype=jnp.int32)[None, :] - my_start[:, None]
    live_rows = offsets < my_count[:, None]
    masked = jnp.where(live_rows.reshape(tok_rows, 1, 1), out_grad, jnp.zeros_like(out_grad))
    masked_flat = masked.reshape(tok_rows, 2 * kv_total)
    masked_own = lax.dynamic_slice_in_dim(masked, shard_index * kv_local, kv_local, 2)
    gradient_block_list = masked_own.reshape(blk_dev, BLK, 2, kv_local)
    weight_full, up_all = (
        lax.all_gather(base_weight, "seq", axis=0, tiled=True),
        lax.all_gather(adapter_up, "seq", axis=0, tiled=True),
    )
    base_term = jnp.dot(masked_flat, weight_full, preferred_element_type=jnp.float32)
    own_select = (my_slot[:, None] == tenant_ids[None, :]).astype(jnp.bfloat16)
    up_projection_blocks = jnp.einsum(
        "bt,tjrk->bjrk", own_select, up_all, preferred_element_type=jnp.float32
    ).astype(jnp.bfloat16)
    low_part = jnp.einsum(
        "zpex,zehx->zpeh",
        gradient_block_list,
        up_projection_blocks,
        preferred_element_type=jnp.float32,
    ).reshape(tok_rows, rank_width)
    reduced_rank_sum = lax.psum(low_part, ("tensor", "sub"))
    reduced_rank_mine = (adapter_scale_factor * reduced_rank_sum).astype(jnp.bfloat16)
    lowrank_all = lax.all_gather(reduced_rank_mine, "seq", axis=0, tiled=True)
    mid_blocks = adapter_mid.reshape(blk_dev, BLK, 2, rank_width // 2)
    up_projection_share = adapter_scale_factor * jnp.einsum(
        "bqjr,bqjk->bjrk", mid_blocks, gradient_block_list, preferred_element_type=jnp.float32
    )
    block_select = (my_slot[:, None] == tenant_ids[None, :]).astype(jnp.float32)
    up_grad = lax.psum_scatter(
        jnp.einsum(
            "on,olqp->nlqp", block_select, up_projection_share, precision=highest_precision_mode
        ),
        "seq",
        scatter_dimension=0,
        tiled=True,
    )
    up_adapter_gradient = up_grad.astype(jnp.bfloat16)
    input_cols = layer_input.reshape(tok_rows, seq_count, piece_cols)
    down_cols = adapter_down.reshape(ten_dev, seq_count, piece_cols, rank_width)
    feat_rows, down_feat = (
        lax.all_to_all(input_cols, "seq", split_axis=1, concat_axis=0, tiled=True),
        lax.all_to_all(down_cols, "seq", split_axis=1, concat_axis=0, tiled=True),
    )
    feat_blocks = feat_rows.reshape(blocks, BLK, piece_cols)
    down_feat = down_feat.reshape(tenants, piece_cols, rank_width)
    low_blocks = lowrank_all.reshape(blocks, BLK, rank_width)
    adapter_slot_choice = slot_all[:, None] == tenant_ids[None, :]
    down_projection_share = jnp.einsum(
        "bqc,bqr->bcr", feat_blocks, low_blocks, preferred_element_type=jnp.float32
    )
    down_grad = jnp.einsum(
        "bt,bcr->tcr",
        adapter_slot_choice.astype(jnp.float32),
        down_projection_share,
        precision=highest_precision_mode,
    ).astype(jnp.bfloat16)
    down_projection_blocks = jnp.einsum(
        "bt,tcr->bcr",
        adapter_slot_choice.astype(jnp.bfloat16),
        down_feat,
        preferred_element_type=jnp.float32,
    ).astype(jnp.bfloat16)
    side_feat = jnp.einsum(
        "bqr,bcr->bqc", low_blocks, down_projection_blocks, preferred_element_type=jnp.float32
    ).astype(jnp.bfloat16)
    grad_down, adapter_side_term = (
        lax.all_to_all(
            down_grad.reshape(seq_count, ten_dev, piece_cols, rank_width),
            "seq",
            split_axis=0,
            concat_axis=2,
            tiled=True,
        ),
        lax.all_to_all(
            side_feat.reshape(seq_count, tok_rows, piece_cols),
            "seq",
            split_axis=0,
            concat_axis=2,
            tiled=True,
        ),
    )
    grad_input = (
        base_term + adapter_side_term.reshape(tok_rows, width_local).astype(jnp.float32)
    ).astype(jnp.bfloat16)
    return (grad_input, grad_down.reshape(ten_dev, width_local, rank_width), up_adapter_gradient)


MESH = pl.DeviceIdType.MESH
CHUNKS = 2
F32 = jnp.float32
BF16 = jnp.bfloat16


def hosting(planes, tok_blocks):
    blocks, tenants = planes * tok_blocks, planes * 2
    low, high = [], []
    for s in range(planes):
        first, last = s * tok_blocks, (s + 1) * tok_blocks - 1
        least = max(first // tok_blocks, first - (blocks - tenants))
        most = min(last, tenants - 1 - (blocks - 1 - last) // tok_blocks)
        if least < planes:
            low.append(s)
        if most >= planes:
            high.append(s)
    return max(low), min(high)


def line_kernel(
    S, T, C,
    counts, starts, owners,
    x_hbm, og_hbm, mid, w_hbm, dn_hbm, up_hbm,
    gi, gd, gu,
    x, og, w, dn, up, low, gown, gright, gleft, mix, uown, uright, uleft, masked, lsel, msel,
    copy_sem, up_s, up_r, low_s, low_r,
    w_s, w_r, y_s, y_r, dn_s, dn_r, g_s, g_r, u_s, u_r,
):
    s = lax.axis_index("seq")
    g = lax.axis_index("groups")
    t = lax.axis_index("tensor")
    c = lax.axis_index("sub")
    M = T * C
    m = t * C + c
    rows, width = x_hbm.shape
    depth = w_hbm.shape[0]
    half = depth // 2
    piece = half // CHUNKS
    kv_local = up_hbm.shape[3]
    kv = kv_local * M
    nblk = rows // BLK
    N = 2 * S
    rank2 = mid.shape[1]
    rank = rank2 // 2
    last0, first1 = hosting(S, nblk)
    right, left = {"seq": s + 1}, {"seq": s - 1}

    def stage(axis):
        size, index = (C, c) if axis == "sub" else (T, t)
        for k in range(1, size):
            yield k, {axis: lax.rem(index + k, size)}, lax.rem(index + size - k, size)

    def remote(src, dst, send, recv, dev):
        return pltpu.make_async_remote_copy(
            src_ref=src, dst_ref=dst, send_sem=send, recv_sem=recv, device_id=dev, device_id_type=MESH
        )

    own = (
        pltpu.make_async_copy(w_hbm, w.at[pl.ds(s * depth, depth)], copy_sem.at[0]),
        pltpu.make_async_copy(dn_hbm, dn.at[pl.ds(2 * s, 2)], copy_sem.at[1]),
        pltpu.make_async_copy(up_hbm, up.at[pl.ds(2 * s, 2)], copy_sem.at[2]),
    )
    late = (
        pltpu.make_async_copy(og_hbm, og, copy_sem.at[3]),
        pltpu.make_async_copy(x_hbm, x, copy_sem.at[4]),
    )
    for cp in own + late:
        cp.start()

    barrier = pltpu.get_barrier_semaphore()
    for k in range(1, S):
        pl.semaphore_signal(barrier, inc=1, device_id={"seq": lax.rem(s + k, S)}, device_id_type=MESH)
    pl.semaphore_signal(barrier, inc=1, device_id={"groups": 1 - g}, device_id_type=MESH)
    for axis in ("sub", "tensor"):
        for _, dev, _ in stage(axis):
            pl.semaphore_signal(barrier, inc=1, device_id=dev, device_id_type=MESH)
    pl.semaphore_wait(barrier, S - 1 + 1 + C - 1 + T - 1)
    for cp in own:
        cp.wait()

    def up_copy(k, plane, target, j):
        part = up.at[2 * plane + j]
        return remote(part, part, up_s.at[k - 1, j], up_r.at[k - 1, j], {"seq": target})

    def wants(plane, j):
        return plane <= last0 if j == 0 else plane >= first1

    def ups(act):
        for k in range(1, S):
            for j in range(2):
                ahead, behind = lax.rem(s + k, S), lax.rem(s + S - k, S)
                if act == "recv":

                    @pl.when(wants(s, j))
                    def _(k=k, j=j, behind=behind):
                        up_copy(k, behind, s, j).wait_recv()

                else:

                    @pl.when(wants(ahead, j))
                    def _(k=k, j=j, ahead=ahead):
                        cp = up_copy(k, s, ahead, j)
                        cp.start() if act == "start" else cp.wait_send()

    ups("start")

    def w_rows(plane, hlf, i):
        return w.at[pl.ds(pl.multiple_of(plane * depth + hlf * half + i * piece, 16), piece)]

    def origin(way, k):
        return s - k if way == 0 else s + k

    def held(plane):
        return jnp.logical_and(plane >= 0, plane < S)

    def w_copy(way, k, plane, i):
        part = w_rows(plane, g, i)
        return remote(part, part, w_s.at[way, k - 1, i], w_r.at[way, k - 1, i], left if way else right)

    def y_copy(way, k, plane, i, hlf):
        part = w_rows(plane, hlf, i)
        return remote(part, part, y_s.at[way, k - 1, i], y_r.at[way, k - 1, i], {"groups": 1 - g})

    def dn_copy(way, k, plane, j):
        part = dn.at[2 * plane + j]
        return remote(part, part, dn_s.at[way, k - 1, j], dn_r.at[way, k - 1, j], left if way else right)

    def can_send(way, k, j=None):
        plane = origin(way, k - 1)
        nxt = s - 1 if way else s + 1
        ok = jnp.logical_and(held(plane), held(nxt))
        if j == 0:
            ok = jnp.logical_and(ok, nxt <= last0)
        if j == 1:
            ok = jnp.logical_and(ok, nxt >= first1)
        return ok

    def can_recv(way, k, j=None):
        ok = held(origin(way, k))
        if j == 0:
            ok = jnp.logical_and(ok, s <= last0)
        if j == 1:
            ok = jnp.logical_and(ok, s >= first1)
        return ok

    def send_w(k, way, i):
        @pl.when(can_send(way, k))
        def _():
            w_copy(way, k, origin(way, k - 1), i).start()

    cut = (S // 2 - 1, S // 2)

    def tenant_of(block):
        index = jnp.int32(-1)
        for n in range(N):
            index = index + jnp.where(starts[n] <= block * BLK, 1, 0).astype(jnp.int32)
        return index

    takes_grads = (tenant_of(S // 2 * nblk - 1) >= S, tenant_of(S // 2 * nblk) < S)

    def mix_copy(k, way):
        to = dn.at[2 * origin(way, k - 1) + way]
        dev = left if way else right
        return remote(mix.at[way, k - 1], to, dn_s.at[way, k - 1, way], dn_r.at[way, k - 1, way], dev)

    def dn_sends(k, way, j, act):
        ok = can_send(way, k, j)
        if j == way:

            @pl.when(jnp.logical_and(ok, s == cut[way]))
            def _():
                if act == "wait":
                    mix_copy(k, way).wait_send()

            ok = jnp.logical_and(ok, s != cut[way])

        @pl.when(ok)
        def _():
            cp = dn_copy(way, k, origin(way, k - 1), j)
            cp.wait_send() if act == "wait" else cp.start()

    def send_dn(k, way, j):
        dn_sends(k, way, j, "start")

    def mixed_dest(way, k):
        return k - 1 if way else S - k

    def mixed(way, plane, j):
        return plane == cut[way] and j != way

    def send_mix(k, way):
        @pl.when(s == cut[way])
        def _():
            hit = jnp.where(takes_grads[way], 1.0, 0.0).astype(F32)
            own_map = 2 * origin(way, k - 1) + way
            n = 2 * mixed_dest(way, k) + 1 - way

            @pl.loop(0, width // 256)
            def _(i):
                at = pl.ds(pl.multiple_of(i * 256, 256), 256)
                value = gown[n, at, :].astype(F32) * hit + dn[own_map, at, :].astype(F32) * (1.0 - hit)
                mix[way, k - 1, at, :] = value.astype(BF16)

            mix_copy(k, way).start()

    for i in range(CHUNKS):
        for way in range(2):
            send_w(1, way, i)
    for j in range(2):
        for way in range(2):
            send_dn(1, way, j)

    for p in range(S):
        for j in range(2):
            unused = s > last0 if j == 0 else s < first1

            @pl.when(jnp.logical_and(unused, s != p))
            def _(p=p, j=j):
                dn[2 * p + j] = jnp.zeros(dn.shape[1:], dn.dtype)

    for cp in late:
        cp.wait()
    slots = []
    for b in range(nblk):
        first = (s * nblk + b) * BLK
        tenant = jnp.int32(-1)
        for n in range(N):
            tenant = tenant + jnp.where(starts[n] <= first, 1, 0).astype(jnp.int32)
        live = counts[tenant] - (first - starts[tenant])
        slots.append(owners[tenant])
        here = pl.ds(b * BLK, BLK)
        keep = lax.broadcasted_iota(jnp.int32, (BLK, kv), 0) < live
        for j in range(2):
            value = og[here, j, :].astype(F32)
            masked[here, j * kv : (j + 1) * kv] = jnp.where(keep, value, 0.0).astype(BF16)

    def own_features(j):
        return pl.ds(pl.multiple_of(j * kv + m * kv_local, 128), kv_local)

    ups("recv")
    for b in range(nblk):
        here = pl.ds(b * BLK, BLK)
        for j in range(2):
            low[c, here, j * rank : (j + 1) * rank] = lax.dot_general(
                masked[here, own_features(j)],
                up[slots[b], j],
                (((1,), (1,)), ((), ())),
                preferred_element_type=F32,
            )

    def low_copy(k, index, dev, first):
        return remote(
            low.at[first + index], low.at[first + index], low_s.at[first + k - 1], low_r.at[first + k - 1], dev
        )

    for k, dev, _ in stage("sub"):
        low_copy(k, c, dev, 0).start()
    for k, dev, behind in stage("sub"):
        low_copy(k, behind, dev, 0).wait_recv()
    chip_sum = low[0]
    for q in range(1, C):
        chip_sum = chip_sum + low[q]
    low[C + t] = chip_sum
    for k, dev, _ in stage("tensor"):
        low_copy(k, t, dev, C).start()

    for b in range(nblk):
        here = pl.ds(b * BLK, BLK)
        value = mid[here, :].astype(F32)
        for n in range(N):
            hit = jnp.where(slots[b] == n, 1.0, 0.0).astype(F32)
            msel[here, n * rank2 : (n + 1) * rank2] = (value * hit).astype(BF16)
    for n in range(N):
        both = msel[:, n * rank2 : (n + 1) * rank2]
        for j in range(2):
            share = lax.dot_general(
                both, masked[:, own_features(j)], (((0,), (0,)), ((), ())), preferred_element_type=F32
            )
            uown[n, j] = (adapter_scale_factor * share[j * rank : (j + 1) * rank, :]).astype(BF16)

    for k, dev, behind in stage("tensor"):
        low_copy(k, behind, dev, C).wait_recv()
    total = low[C]
    for q in range(1, T):
        total = total + low[C + q]
    lowrank = (adapter_scale_factor * total).astype(BF16).astype(F32)
    for b in range(nblk):
        here = pl.ds(b * BLK, BLK)
        value = lowrank[b * BLK : (b + 1) * BLK, :]
        for n in range(N):
            hit = jnp.where(slots[b] == n, 1.0, 0.0).astype(F32)
            lsel[here, n * rank2 : (n + 1) * rank2] = (value * hit).astype(BF16)

    def hop_w(k):
        for i in range(CHUNKS):
            for way in range(2):

                @pl.when(can_recv(way, k))
                def _(way=way, i=i):
                    w_copy(way, k, origin(way, k), i).wait_recv()
                    if k < S - 1:
                        send_w(k + 1, way, i)
                    y_copy(way, k, origin(way, k), i, g).start()

    def hop_dn(k):
        for j in range(2):
            for way in range(2):

                @pl.when(can_recv(way, k, j))
                def _(way=way, j=j):
                    dn_copy(way, k, origin(way, k), j).wait_recv()
                    if k < S - 1:
                        send_dn(k + 1, way, j)

                if j == way and k < S // 2:
                    send_mix(k + 1, way)

    def hop(k):
        hop_w(k)
        hop_dn(k)

    hop_w(1)
    step = 256

    @pl.loop(0, width // step)
    def _(i):
        at = pl.ds(pl.multiple_of(i * step, step), step)
        share = lax.dot_general(
            x[:, at], lsel[...], (((0,), (0,)), ((), ())), preferred_element_type=F32
        )
        for n in range(N):
            gown[n, at, :] = share[:, n * rank2 : (n + 1) * rank2].astype(BF16)

    g_in, u_in = (gright, gleft), (uright, uleft)

    def grad_copies(way, sender, d, j):
        n = 2 * d + j
        dev = left if way else right
        small = remote(uown.at[n], u_in[way].at[n], u_s.at[n], u_r.at[way, n], dev)
        if mixed(way, sender, j):
            return (small,)
        return (remote(gown.at[n], g_in[way].at[n], g_s.at[n], g_r.at[way, n], dev), small)

    def gives(way, plane, j):
        if way == 0:
            return plane >= (0 if j == 0 else first1)
        return plane <= (last0 if j == 0 else S - 1)

    def add_in(way, sender, d, j):
        n = 2 * d + j
        came, scale = g_in[way].at[n], None
        if mixed(way, sender, j):
            k = d + 1 if way else S - d
            came = dn.at[2 * (sender + k - 1 if way else sender - k + 1) + way]
            scale = jnp.where(takes_grads[way], 1.0, 0.0).astype(F32)

        @pl.loop(0, width // step)
        def _(i):
            at = pl.ds(pl.multiple_of(i * step, step), step)
            value = came[at, :].astype(F32)
            if scale is not None:
                value = value * scale
            gown[n, at, :] = (gown[n, at, :].astype(F32) + value).astype(BF16)

        uown[n] = (uown[n].astype(F32) + u_in[way][n].astype(F32)).astype(BF16)

    def grad_turn(way, plane, alone):
        @pl.when(s == plane)
        def _():
            behind = plane + 1 if way else plane - 1
            dests = range(plane - 1, -1, -1) if way else range(plane + 1, S)
            for d in reversed(dests):
                for j in range(2):
                    joined = 0 <= behind < S and gives(way, behind, j)
                    if joined != alone and gives(way, plane, j):
                        if joined:
                            for cp in grad_copies(way, behind, d, j):
                                cp.wait_recv()
                            add_in(way, behind, d, j)
                        for cp in grad_copies(way, plane, d, j):
                            cp.start()

    def grad_end(plane):
        @pl.when(s == plane)
        def _():
            for way in range(2):
                behind = plane + 1 if way else plane - 1
                for j in range(2):
                    if 0 <= behind < S and gives(way, behind, j):
                        for cp in grad_copies(way, behind, plane, j):
                            cp.wait_recv()
                        add_in(way, behind, plane, j)

    for way in range(2):
        send_mix(1, way)
    grad_turn(0, 0, True)
    grad_turn(1, S - 1, True)
    hop_dn(1)
    for p in range(1, S - 1):
        grad_turn(0, p, True)
        grad_turn(1, S - 1 - p, True)
    grad_turn(0, 1, False)
    grad_turn(1, S - 2, False)
    for k in range(2, S - 1):
        hop(k)
    for p in range(2, S - 1):
        grad_turn(0, p, False)
        grad_turn(1, S - 1 - p, False)
    if S > 2:
        hop(S - 1)

    for k in range(1, S):
        for i in range(CHUNKS):
            for way in range(2):

                @pl.when(can_recv(way, k))
                def _(way=way, i=i, k=k):
                    y_copy(way, k, origin(way, k), i, 1 - g).wait_recv()

    @pl.loop(0, width // step)
    def _(i):
        at = pl.ds(pl.multiple_of(i * step, step), step)
        base = jnp.dot(masked[...], w[:, at], preferred_element_type=F32)
        side = jnp.zeros((rows, step), F32)
        for n in range(N):
            side = side + lax.dot_general(
                lsel[:, n * rank2 : (n + 1) * rank2],
                dn[n, at, :],
                (((1,), (1,)), ((), ())),
                preferred_element_type=F32,
            )
        gi[:, at] = (base + side.astype(BF16).astype(F32)).astype(BF16)

    for p in range(S):
        grad_end(p)
    gd[...] = gown[pl.ds(2 * s, 2)]
    gu[...] = uown[pl.ds(2 * s, 2)]

    ups("wait")
    for k, dev, _ in stage("sub"):
        low_copy(k, c, dev, 0).wait_send()
    for k, dev, _ in stage("tensor"):
        low_copy(k, t, dev, C).wait_send()
    for k in range(1, S):
        for way in range(2):
            for i in range(CHUNKS):

                @pl.when(can_send(way, k))
                def _(k=k, way=way, i=i):
                    w_copy(way, k, origin(way, k - 1), i).wait_send()

                @pl.when(can_recv(way, k))
                def _(k=k, way=way, i=i):
                    y_copy(way, k, origin(way, k), i, g).wait_send()

            for j in range(2):

                dn_sends(k, way, j, "wait")

    for plane in range(S):

        @pl.when(s == plane)
        def _(plane=plane):
            for d in range(S):
                for j in range(2):
                    way = 0 if d > plane else 1
                    if d != plane and gives(way, plane, j):
                        for cp in grad_copies(way, plane, d, j):
                            cp.wait_send()


def line_local(S, T, C, layer_input, out_grad, base_weight, adapter_mid, adapter_down, adapter_up,
               tenant_counts, seg_starts, owner_slot):
    rows, width = layer_input.shape
    N = 2 * S
    rank2 = adapter_down.shape[2]
    kv2 = 2 * out_grad.shape[2]
    up_shape = adapter_up.shape[1:]
    vmem = pl.BlockSpec(memory_space=pltpu.VMEM)
    smem = pl.BlockSpec(memory_space=pltpu.SMEM)
    hbm = pl.BlockSpec(memory_space=pl.ANY)
    dma = pltpu.SemaphoreType.DMA
    grads = pltpu.VMEM((N, width, rank2), BF16)
    ups = pltpu.VMEM((N,) + up_shape, BF16)
    return pl.pallas_call(
        functools.partial(line_kernel, S, T, C),
        out_shape=(
            jax.ShapeDtypeStruct((rows, width), BF16),
            jax.ShapeDtypeStruct(adapter_down.shape, BF16),
            jax.ShapeDtypeStruct(adapter_up.shape, BF16),
        ),
        in_specs=[smem] * 3 + [hbm] * 2 + [vmem] + [hbm] * 3,
        out_specs=(vmem, vmem, vmem),
        scratch_shapes=[
            pltpu.VMEM((rows, width), BF16),
            pltpu.VMEM(out_grad.shape, BF16),
            pltpu.VMEM((S * base_weight.shape[0], width), BF16),
            grads,
            ups,
            pltpu.VMEM((C + T, rows, rank2), F32),
            grads, grads, grads,
            pltpu.VMEM((2, S // 2, width, rank2), BF16),
            ups, ups, ups,
            pltpu.VMEM((rows, kv2), BF16),
            pltpu.VMEM((rows, N * rank2), BF16),
            pltpu.VMEM((rows, N * rank2), BF16),
            dma((5,)),
            dma((S - 1, 2)), dma((S - 1, 2)),
            dma((C + T,)), dma((C + T,)),
            dma((2, S - 1, CHUNKS)), dma((2, S - 1, CHUNKS)),
            dma((2, S - 1, CHUNKS)), dma((2, S - 1, CHUNKS)),
            dma((2, S - 1, 2)), dma((2, S - 1, 2)),
            dma((N,)), dma((2, N)),
            dma((N,)), dma((2, N)),
        ],
        compiler_params=pltpu.CompilerParams(
            collective_id=0, has_side_effects=True, vmem_limit_bytes=58 * 1024 * 1024
        ),
        name="line",
    )(
        tenant_counts, seg_starts, owner_slot,
        layer_input, out_grad, adapter_mid, base_weight, adapter_down, adapter_up,
    )


def solution(mesh):
    S, T, C = mesh.shape["seq"], mesh.shape["tensor"], mesh.shape["sub"]
    short = S == 4 and mesh.shape["groups"] == 2
    body = functools.partial(line_local, S, T, C) if short else local

    return jax.shard_map(
        body,
        mesh=mesh,
        in_specs=(
            P(("groups", "seq"), ("tensor", "sub")),
            P(("groups", "seq"), None, None),
            P("seq", ("tensor", "sub")),
            P(("groups", "seq"), None),
            P(("groups", "seq"), ("tensor", "sub"), None),
            P(("groups", "seq"), None, None, ("tensor", "sub")),
            P("groups"),
            P("groups"),
            P("groups"),
        ),
        out_specs=(
            P(("groups", "seq"), ("tensor", "sub")),
            P(("groups", "seq"), ("tensor", "sub"), None),
            P(("groups", "seq"), None, None, ("tensor", "sub")),
        ),
        check_vma=False,
    )
```
